32 devices in a mesh: groups: 2 (over x), seq: 16 (over z, y, core).
Axes of the slice: x: 2, y: 2, z: 4, core: 2. Of those that a mesh axis runs over, the one named last changes fastest.
Arguments:
- queries: bfloat16 [12288, 4096], P(('groups', 'seq')), parts along dimension 0, may hold values from -1.796875 to 1.796875
- keys: bfloat16 [12288, 4096], P(('groups', 'seq')), parts along dimension 0, may hold values from -1.796875 to 1.796875
- values: bfloat16 [12288, 4096], P(('groups', 'seq')), parts along dimension 0, may hold values from -1.796875 to 1.796875
- out_grad: bfloat16 [12288, 4096], P(('groups', 'seq')), parts along dimension 0, may hold values from -0.59765625 to 0.59765625
- decay_rate: float32 [32, 12288], P(None, ('groups', 'seq')), parts along dimension 1, may hold values from 0 to 1
- block_parent: int32 [32], P('groups'), parts along dimension 0, may hold values from -1 to 14, as said below
- block_valid: int32 [32], P('groups'), parts along dimension 0, may hold values from 96 to 384, as said below
Outputs:
- query_grad: bfloat16 [12288, 4096], P(('groups', 'seq')), parts along dimension 0
- key_grad: bfloat16 [12288, 4096], P(('groups', 'seq')), parts along dimension 0
- value_grad: bfloat16 [12288, 4096], P(('groups', 'seq')), parts along dimension 0
The draws below stay inside these ranges and needn't reach their ends.
There are 2 independent parts, one for each index of `groups`. The reference program is written for one: setup_inputs(seed, part) draws one part's arguments, and reference() takes and returns one part's arrays. A program takes and returns all parts, laid end to end along the dimension named above; each array names one. Nothing has to cross between parts.
Inputs may be any that keep to these rules, and one draw needn't show every extreme that they name: `block_parent`: blocks 0 to 3 hold the prompt in order: block c has parent c - 1, block 0 has -1. The other blocks hold 8 branches, each a run of 1 to 4 consecutive blocks, in order of their first block; a branch's first block has parent 4 - 1 and its other blocks have parent c - 1. Block 4 starts a branch, at least one branch has exactly 4 blocks and no branch has more, and the last branch has 2 or more. `block_valid`: 384 for every block except the last block of each branch.
All inputs are finite; a program needn't handle non-finite values.
Results may differ from the reference program's by a relative error of at most 0.0057.
Values sent between devices are 32-bit elements; how exact they have to be, the bound alone decides.
A program may use at most 448 MiB of HBM per device.

```python
import jax
import jax.numpy as jnp
from jax import lax

HEADS = 32
HD = 128
SEGMENT_LENGTH = 384
BLOCKS = 16
PROMPT_BLOCKS = 4
ROLLOUT_TALLY = 8
CLUSTER_LENGTH = 6144
WIDTH = 4096
CHAIN = 3072


def branch_sizes(key):
    extra = BLOCKS - PROMPT_BLOCKS - ROLLOUT_TALLY - 4
    pick_key, spread_key = jax.random.split(key)
    rollout_indices_list = jnp.arange(ROLLOUT_TALLY)
    maximal_rollout = jax.random.randint(pick_key, (), 0, ROLLOUT_TALLY)
    extra_index_slot = jnp.where(maximal_rollout == ROLLOUT_TALLY - 1, 0, ROLLOUT_TALLY - 1)
    present_lengths = 1 + 3 * (rollout_indices_list == maximal_rollout).astype(jnp.int32) + (rollout_indices_list == extra_index_slot).astype(jnp.int32)
    spread_keys = jax.random.split(spread_key, max(extra, 1))
    for step_no in range(extra):
        jitter = jax.random.randint(spread_keys[step_no], (ROLLOUT_TALLY,), 0, 4096)
        ranking = (present_lengths < 4).astype(jnp.int32) * (4096 * ROLLOUT_TALLY) + jitter * ROLLOUT_TALLY + rollout_indices_list
        chosen = lax.top_k(ranking, 1)[1][0]
        present_lengths = present_lengths + (rollout_indices_list == chosen).astype(jnp.int32)
    starts = PROMPT_BLOCKS + jnp.cumsum(present_lengths) - present_lengths
    return (starts, starts + present_lengths - 1)


def draw_block_parent(key, part):
    starts, finals = branch_sizes(key)
    indices = jnp.arange(BLOCKS)
    opening = jnp.any(indices[:, None] == starts[None, :], axis=1)
    return jnp.where(opening, PROMPT_BLOCKS - 1, indices - 1).astype(jnp.int32)


def draw_block_valid(key, part):
    starts, finals = branch_sizes(key)
    key = jax.random.fold_in(key, 5)
    tail_key, short_key = jax.random.split(key)
    tails = jax.random.randint(tail_key, (ROLLOUT_TALLY,), SEGMENT_LENGTH // 4, SEGMENT_LENGTH + 1)
    shortest = jax.random.randint(short_key, (), 0, ROLLOUT_TALLY)
    tails = jnp.where(jnp.arange(ROLLOUT_TALLY) == shortest, SEGMENT_LENGTH // 4, tails)
    indices = jnp.arange(BLOCKS)
    closing = indices[:, None] == finals[None, :]
    tail_of = jnp.sum(jnp.where(closing, tails[None, :], 0), axis=1)
    return jnp.where(jnp.any(closing, axis=1), tail_of, SEGMENT_LENGTH).astype(jnp.int32)


def draw_decay_rate(key, part):
    key = jax.random.fold_in(key, 7)
    initial_seed, multiplier_seed, spike_seed, magnitude_seed = jax.random.split(key, 4)
    slowest = 0.3 / CHAIN
    per_head = jnp.exp(jax.random.uniform(initial_seed, (HEADS,), jnp.float32, jnp.log(slowest), jnp.log(1.0 / 30.0)))
    factor = jnp.exp(jax.random.uniform(multiplier_seed, (HEADS, BLOCKS, 1), jnp.float32, jnp.log(0.6), jnp.log(1.6)))
    forget_speed_lines = (per_head[:, None, None] * factor * jnp.ones((1, 1, SEGMENT_LENGTH), jnp.float32)).reshape(HEADS, CLUSTER_LENGTH)
    spike_index_slot = jax.random.uniform(spike_seed, (1, CLUSTER_LENGTH)) < 0.5 / SEGMENT_LENGTH
    overall_magnitude = jax.random.uniform(magnitude_seed, (1, CLUSTER_LENGTH), jnp.float32, 0.22, 0.69)
    return forget_speed_lines + jnp.where(spike_index_slot, overall_magnitude, 0.0)


def steps_of(own_key, dims, cuts, least, largest):
    def one(dim, shards_of):
        heights = jax.random.uniform(jax.random.fold_in(jax.random.fold_in(own_key, 6), dim), (shards_of,), jnp.float32, least / len(cuts), largest / len(cuts))
        return jnp.repeat(jnp.exp(heights), dims[dim] // shards_of).reshape((-1,) + (1,) * (len(dims) - dim - 1))

    level = one(*cuts[0])
    for cut in cuts[1:]:
        level = level * one(*cut)
    return level


def noise(key, extent, spread, most, cuts=(), kind=jnp.bfloat16):
    loudness = steps_of(key, extent, cuts, -0.22, 0.18) if cuts else 1.0
    values = jax.random.normal(key, extent, jnp.float32) * spread * loudness
    return jnp.minimum(jnp.maximum(values, -most), most).astype(kind)


def setup_inputs(seed: int = 0, part: int = 0) -> dict:
    key_list = jax.random.split(jax.random.key(seed), 8)
    part_keys = jax.random.split(jax.random.fold_in(key_list[7], part), 8)
    return {
        "queries": noise(part_keys[0], (CLUSTER_LENGTH, WIDTH), 0.3, 1.796875, ((0, 16),)),
        "keys": noise(part_keys[1], (CLUSTER_LENGTH, WIDTH), 0.3, 1.796875, ((0, 16),)),
        "values": noise(part_keys[2], (CLUSTER_LENGTH, WIDTH), 0.3, 1.796875, ((0, 16),)),
        "out_grad": noise(part_keys[3], (CLUSTER_LENGTH, WIDTH), 0.1, 0.59765625, ((0, 16),)),
        "decay_rate": draw_decay_rate(jax.random.fold_in(jax.random.fold_in(key_list[7], part), 71), part),
        "block_parent": draw_block_parent(jax.random.fold_in(jax.random.fold_in(key_list[7], part), 71), part),
        "block_valid": draw_block_valid(jax.random.fold_in(jax.random.fold_in(key_list[7], part), 71), part),
    }


def masked_inputs(queries, keys, values, out_grad, decay_rate, block_valid):
    row_pos = jnp.arange(CLUSTER_LENGTH) % SEGMENT_LENGTH
    row_limit = jnp.repeat(block_valid, SEGMENT_LENGTH)
    live_rows = row_pos < row_limit
    zero_bf = jnp.zeros((), jnp.bfloat16)

    def shaped(matrix):
        return jnp.where(live_rows[:, None], matrix, zero_bf).reshape(BLOCKS, SEGMENT_LENGTH, HEADS, HD)

    log_decay = jnp.where(live_rows[None, :], -decay_rate, jnp.zeros((), jnp.float32))
    log_decay = log_decay.reshape(HEADS, BLOCKS, SEGMENT_LENGTH).transpose(1, 0, 2)
    cumulative = jnp.cumsum(log_decay, axis=2)
    return shaped(queries), shaped(keys), shaped(values), shaped(out_grad), cumulative


def rounded(matrix):
    return lax.optimization_barrier(matrix.astype(jnp.bfloat16)).astype(jnp.float32)


def block_loads(pieces):
    query_blk, key_blk, value_blk, grad_blk, cumulative = pieces
    tail_w = jnp.exp(cumulative[:, -1:] - cumulative)
    head_w = jnp.exp(cumulative)
    key_w = rounded(tail_w.T[:, :, None] * key_blk.astype(jnp.float32))
    query_w = rounded(head_w.T[:, :, None] * query_blk.astype(jnp.float32))
    local_state = jnp.einsum("shd,she->hde", key_w, value_blk.astype(jnp.float32))
    state_grad = jnp.einsum("thd,the->hde", query_w, grad_blk.astype(jnp.float32))
    return jnp.exp(cumulative[:, -1]), local_state, state_grad


def block_grads(pieces):
    query_blk, key_blk, value_blk, grad_blk, cumulative, state_in, grad_out = pieces
    query_f = query_blk.astype(jnp.float32)
    key_f = key_blk.astype(jnp.float32)
    value_f = value_blk.astype(jnp.float32)
    grad_f = grad_blk.astype(jnp.float32)
    tail_w = jnp.exp(cumulative[:, -1:] - cumulative)
    head_w = jnp.exp(cumulative)
    scores = jnp.einsum("thd,shd->hts", query_f, key_f)
    grad_dots = jnp.einsum("the,she->hts", grad_f, value_f)
    log_gaps = cumulative[:, :, None] - cumulative[:, None, :]
    causal = jnp.arange(SEGMENT_LENGTH)[:, None] >= jnp.arange(SEGMENT_LENGTH)[None, :]
    weights = jnp.where(causal[None], jnp.exp(jnp.minimum(log_gaps, 0.0)), 0.0)
    attn_mix = rounded(scores * weights)
    grad_mix = rounded(grad_dots * weights)
    state_bf = rounded(state_in)
    grad_bf = rounded(grad_out)
    query_out = jnp.einsum("hts,shd->thd", grad_mix, key_f) + head_w.T[:, :, None] * jnp.einsum("the,hde->thd", grad_f, state_bf)
    key_out = jnp.einsum("hts,thd->shd", grad_mix, query_f) + tail_w.T[:, :, None] * jnp.einsum("she,hde->shd", value_f, grad_bf)
    value_out = jnp.einsum("hts,the->she", attn_mix, grad_f) + tail_w.T[:, :, None] * jnp.einsum("shd,hde->she", key_f, grad_bf)
    return (query_out.astype(jnp.bfloat16).reshape(SEGMENT_LENGTH, WIDTH),
            key_out.astype(jnp.bfloat16).reshape(SEGMENT_LENGTH, WIDTH),
            value_out.astype(jnp.bfloat16).reshape(SEGMENT_LENGTH, WIDTH))


def reference(queries, keys, values, out_grad, decay_rate, block_parent, block_valid):
    query_all, key_all, value_all, grad_all, cumulative = masked_inputs(queries, keys, values, out_grad, decay_rate, block_valid)
    decays, loads, state_grads = lax.map(block_loads, (query_all, key_all, value_all, grad_all, cumulative))
    empty = jnp.zeros((BLOCKS, HEADS, HD, HD), jnp.float32)

    def forward(position, states):
        position = position.astype(jnp.int32)
        parent = block_parent[position].astype(jnp.int32)
        parent_state = lax.dynamic_index_in_dim(states, parent, 0, keepdims=False)
        parent_decay = lax.dynamic_index_in_dim(decays, parent, 0, keepdims=False)
        parent_load = lax.dynamic_index_in_dim(loads, parent, 0, keepdims=False)
        new_state = parent_decay[:, None, None] * parent_state + parent_load
        return lax.dynamic_update_index_in_dim(states, new_state, position, 0)

    states = lax.fori_loop(1, BLOCKS, forward, empty)

    def backward(step_no, grads):
        child_block = (BLOCKS - 1 - step_no).astype(jnp.int32)
        parent = block_parent[child_block].astype(jnp.int32)
        child_grad = lax.dynamic_index_in_dim(grads, child_block, 0, keepdims=False)
        child_decay = lax.dynamic_index_in_dim(decays, child_block, 0, keepdims=False)
        child_load = lax.dynamic_index_in_dim(state_grads, child_block, 0, keepdims=False)
        passed = child_decay[:, None, None] * child_grad + child_load
        held_grad = lax.dynamic_index_in_dim(grads, parent, 0, keepdims=False)
        return lax.dynamic_update_index_in_dim(grads, held_grad + passed, parent, 0)

    grads = lax.fori_loop(0, BLOCKS - 1, backward, empty)
    query_out, key_out, value_out = lax.map(block_grads, (query_all, key_all, value_all, grad_all, cumulative, states, grads))
    return (query_out.reshape(CLUSTER_LENGTH, WIDTH), key_out.reshape(CLUSTER_LENGTH, WIDTH), value_out.reshape(CLUSTER_LENGTH, WIDTH))
```

```python
import functools

import jax
import jax.numpy as jnp
from jax import lax
from jax.experimental import pallas as pl
from jax.experimental.pallas import tpu as pltpu
from jax.sharding import PartitionSpec as P

F32 = jnp.float32
BF16 = jnp.bfloat16
TN = (((0,), (0,)), ((), ()))
NT = (((1,), (1,)), ((), ()))


def dot(a, b, dims=(((1,), (0,)), ((), ())), precision=None):
    return lax.dot_general(a, b, dims, precision=precision, preferred_element_type=F32)


def live_mask(valid, rows, width):
    return (lax.broadcasted_iota(jnp.int32, (rows, width), 0) < valid).astype(F32).astype(BF16)


def head_column(cum_t, head):
    lane = lax.broadcasted_iota(jnp.int32, cum_t.shape, 1)
    return jnp.sum(jnp.where(lane == head, cum_t, 0.0), axis=1, keepdims=True)


def local_kernel(per, valid, rate, q, k, v, g, state, grad, cum, cum_t, decay):
    rows = q.shape[0]
    size = state.shape[1]

    @pl.when(pl.program_id(0) == 0)
    def _():
        place = lax.broadcasted_iota(jnp.int32, rate.shape, 1)
        log_decay = jnp.where(place < valid[0], -rate[...], 0.0)
        below = lax.broadcasted_iota(jnp.int32, (rows, rows), 0) >= lax.broadcasted_iota(
            jnp.int32, (rows, rows), 1
        )
        tri = below.astype(F32)
        high = lax.Precision.HIGHEST
        cum[...] = dot(log_decay, tri, NT, high)
        cum_t[...] = dot(tri, log_decay, NT, high)
        decay[...] = jnp.broadcast_to(jnp.exp(cum[:, rows - 1 : rows]), decay.shape)

    mask = live_mask(valid[0], rows, size)
    for part in range(per):
        head = pl.program_id(0) * per + part
        cols = slice(part * size, (part + 1) * size)
        column = head_column(cum_t[...], head)
        head_w = jnp.exp(column)
        tail_w = jnp.exp(column[rows - 1 :, :] - column)
        key_w = (tail_w * (k[:, cols] * mask).astype(F32)).astype(BF16)
        query_w = (head_w * (q[:, cols] * mask).astype(F32)).astype(BF16)
        state[part] = dot(key_w, v[:, cols] * mask, TN)
        grad[part] = dot(query_w, g[:, cols] * mask, TN)


def grads_kernel(per, valid, cum, cum_t, q, k, v, g, state, grad, dq, dk, dv):
    rows = q.shape[0]
    size = state.shape[1]
    mask = live_mask(valid[0], rows, size)
    causal_t = lax.broadcasted_iota(jnp.int32, (rows, rows), 0) <= lax.broadcasted_iota(
        jnp.int32, (rows, rows), 1
    )
    for part in range(per):
        head = pl.program_id(0) * per + part
        cols = slice(part * size, (part + 1) * size)
        column = head_column(cum_t[...], head)
        row = cum[pl.ds(head, 1), :]
        head_w = jnp.exp(column)
        tail_w = jnp.exp(column[rows - 1 :, :] - column)
        qm, km, vm, gm = (ref[:, cols] * mask for ref in (q, k, v, g))
        weight_t = jnp.where(causal_t, jnp.exp(jnp.minimum(row - column, 0.0)), 0.0)
        attn_t = (dot(km, qm, NT) * weight_t).astype(BF16)
        gmix_t = (dot(vm, gm, NT) * weight_t).astype(BF16)
        dq[:, cols] = (dot(gmix_t, km, TN) + head_w * dot(gm, state[part], NT)).astype(BF16)
        dk[:, cols] = (dot(gmix_t, qm) + tail_w * dot(vm, grad[part], NT)).astype(BF16)
        dv[:, cols] = (dot(attn_t, gm) + tail_w * dot(km, grad[part])).astype(BF16)


def chain_kernel(
    n, prompt, chunk, load, gload, decay, flags, state_out, grad_out,
    r_f, r_e, r_b, r_x, r_y, s_f, s_b, s_x, send_sem, recv_sem,
):
    c = lax.axis_index("seq")
    count = load.shape[0] // chunk
    root = prompt - 1
    branch = c >= prompt
    even = lax.rem(c, 2) == 0
    node = branch & even
    inner = node & (c + 4 < n)
    partners = [
        (c > 0, c - 1),
        (c < n - 1, c + 1),
        (inner, c + 4),
        (node & (c - 4 >= prompt), c - 4),
        (c == prompt + 2, root),
        (c == root, prompt + 2),
    ]
    barrier = pltpu.get_barrier_semaphore()
    total = 0
    for cond, other in partners:
        total = total + cond.astype(jnp.int32)

        @pl.when(cond)
        def _(other=other):
            pl.semaphore_signal(
                barrier, inc=1, device_id={"seq": other}, device_id_type=pl.DeviceIdType.MESH
            )

    pl.semaphore_wait(barrier, total)

    def at(i):
        return pl.ds(i * chunk, chunk)

    def copy(src, dst, si, ri, i, other):
        return pltpu.make_async_remote_copy(
            src_ref=src.at[at(i)],
            dst_ref=dst.at[at(i)],
            send_sem=send_sem.at[si, i],
            recv_sem=recv_sem.at[ri, i],
            device_id={"seq": other},
            device_id_type=pl.DeviceIdType.MESH,
        )

    away = lax.rem(c + 1, n)

    def arrived(ref, ri, i):
        copy(ref, ref, 0, ri, i, away).wait_recv()

    sends = [
        ("e", node, r_e, r_e, 1, 1, c + 1),
        ("e", inner, r_e, r_e, 2, 1, c + 4),
        ("f", (c != root) & (c < n - 1), s_f, r_f, 0, 0, c + 1),
        ("f", c == root, s_f, r_e, 1, 1, c + 1),
        ("f", c == root, s_f, r_e, 2, 1, prompt + 2),
        ("b", (c > 0) & (c != prompt), s_b, r_b, 3, 2, c - 1),
        ("x", node & (c - 4 >= prompt), s_x, r_x, 4, 3, c - 4),
        ("x", c == prompt, s_x, r_x, 4, 3, c - 1),
        ("x", c == prompt + 2, s_x, r_y, 4, 4, root),
    ]

    def dispatch(kind, i):
        for name, cond, src, dst, si, ri, other in sends:
            if name == kind:

                @pl.when(cond)
                def _(src=src, dst=dst, si=si, ri=ri, other=other):
                    copy(src, dst, si, ri, i, other).start()

    own = flags[0:1, :][None] > 0.5
    following = flags[1:2, :][None] > 0.5
    zeros = jnp.zeros((chunk,) + load.shape[1:], F32)
    e_depth = jnp.where(even, prompt + (c - prompt) // 4, prompt + (c - 1 - prompt) // 4 + 1)

    def inside(i):
        return (i >= 0) & (i < count)

    def fade(i):
        return jnp.concatenate(
            [decay[pl.ds(i * chunk + j, 1), :][None] for j in range(chunk)], axis=0
        )

    def step(t, carry):
        ie = t - e_depth

        @pl.when(branch & inside(ie))
        def _():
            arrived(r_e, 1, ie)
            dispatch("e", ie)

        i = t - c

        @pl.when(inside(i))
        def _():
            @pl.when((c > 0) & (c != prompt))
            def _():
                arrived(r_f, 0, i)

            @pl.when((c == 0) | (c == prompt))
            def _():
                r_f[at(i)] = zeros

            @pl.when(c < prompt)
            def _():
                r_e[at(i)] = zeros

            state = jnp.where(own, r_e[at(i)], r_f[at(i)])
            s_f[at(i)] = fade(i) * state + load[at(i)]
            dispatch("f", i)
            state_out[at(i)] = state.astype(BF16)

        k = t - (n - 1 - c)

        @pl.when(inside(k))
        def _():
            @pl.when((c < n - 1) & (c != root))
            def _():
                arrived(r_b, 2, k)

            @pl.when(c == n - 1)
            def _():
                r_b[at(k)] = zeros

            @pl.when(c == root)
            def _():
                arrived(r_x, 3, k)
                arrived(r_y, 4, k)
                r_b[at(k)] = r_x[at(k)] + r_y[at(k)]

            back = r_b[at(k)]
            held = jnp.where(following, 0.0, back)
            onward = fade(k) * held + gload[at(k)]
            s_b[at(k)] = onward
            dispatch("b", k)

            @pl.when(node)
            def _():
                @pl.when(inner)
                def _():
                    arrived(r_x, 3, k)

                @pl.when(jnp.logical_not(inner))
                def _():
                    r_x[at(k)] = zeros

                s_x[at(k)] = (
                    jnp.where(own, onward, 0.0) + jnp.where(following, back, 0.0) + r_x[at(k)]
                )
                dispatch("x", k)

            grad_out[at(k)] = held.astype(BF16)

        return carry

    lax.fori_loop(0, count + n - 1, step, 0)

    def drain(i, carry):
        for name, cond, src, dst, si, ri, other in sends:

            @pl.when(cond)
            def _(src=src, dst=dst, si=si, ri=ri, other=other):
                copy(src, dst, si, ri, i, other).wait_send()

        return carry

    lax.fori_loop(0, count, drain, 0)


def on_device(queries, keys, values, out_grad, decay_rate, block_parent, block_valid):
    rows, width = queries.shape
    heads = decay_rate.shape[0]
    size = width // heads
    n = lax.axis_size("seq")
    prompt = n // 4
    me = lax.axis_index("seq")
    places = jnp.arange(n)
    starts = (places >= prompt) & (block_parent == prompt - 1)
    following = (places == me + 1) & (me != prompt - 1)
    flags = jnp.stack(
        [jnp.any(starts & (places == me)), jnp.any(starts & following)]
    ).astype(F32)
    flags = jnp.broadcast_to(jnp.concatenate([flags, jnp.zeros((6,), F32)])[:, None], (8, size))
    valid = lax.dynamic_slice_in_dim(block_valid, me, 1)

    per = 2
    big = pltpu.CompilerParams(vmem_limit_bytes=48 * 2**20)
    smem = pl.BlockSpec(memory_space=pltpu.SMEM)
    wide = pl.BlockSpec((rows, per * size), lambda i: (0, i))
    mats = pl.BlockSpec((per, size, size), lambda i: (i, 0, 0))

    def whole(*shape):
        return pl.BlockSpec(shape, lambda i: (0,) * len(shape))

    states = jax.ShapeDtypeStruct((heads, size, size), F32)
    load, gload, cum, cum_t, decay = pl.pallas_call(
        functools.partial(local_kernel, per),
        grid=(heads // per,),
        in_specs=[smem, whole(heads, rows), wide, wide, wide, wide],
        out_specs=[mats, mats, whole(heads, rows), whole(rows, heads), whole(heads, size)],
        out_shape=[
            states,
            states,
            jax.ShapeDtypeStruct((heads, rows), F32),
            jax.ShapeDtypeStruct((rows, heads), F32),
            jax.ShapeDtypeStruct((heads, size), F32),
        ],
        compiler_params=big,
        name="local_states",
    )(valid, decay_rate, queries, keys, values, out_grad)

    chunk = 2
    count = heads // chunk
    vmem = pl.BlockSpec(memory_space=pltpu.VMEM)
    state_bf, grad_bf = pl.pallas_call(
        functools.partial(chain_kernel, n, prompt, chunk),
        in_specs=[vmem] * 4,
        out_specs=[vmem] * 2,
        out_shape=[jax.ShapeDtypeStruct((heads, size, size), BF16)] * 2,
        scratch_shapes=[pltpu.VMEM((heads, size, size), F32)] * 8
        + [pltpu.SemaphoreType.DMA((5, count)), pltpu.SemaphoreType.DMA((5, count))],
        compiler_params=pltpu.CompilerParams(
            collective_id=0, has_side_effects=True, vmem_limit_bytes=48 * 2**20
        ),
        name="tree_scan",
    )(load, gload, decay, flags)

    return pl.pallas_call(
        functools.partial(grads_kernel, per),
        grid=(heads // per,),
        in_specs=[smem, whole(heads, rows), whole(rows, heads), wide, wide, wide, wide, mats, mats],
        out_specs=[wide, wide, wide],
        out_shape=[jax.ShapeDtypeStruct((rows, width), BF16)] * 3,
        compiler_params=big,
        name="block_grads",
    )(valid, cum, cum_t, queries, keys, values, out_grad, state_bf, grad_bf)


def solution(mesh):
    rows = P(("groups", "seq"), None)
    placed = (rows, rows, rows, rows, P(None, ("groups", "seq")), P("groups"), P("groups"))
    return jax.shard_map(
        on_device, mesh=mesh, in_specs=placed, out_specs=(rows, rows, rows), check_vma=False
    )
```

```python
import functools

import jax
import jax.numpy as jnp
from jax import lax
from jax.experimental import pallas as pl
from jax.experimental.pallas import tpu as pltpu
from jax.sharding import PartitionSpec as P

F32 = jnp.float32
BF16 = jnp.bfloat16
TN = (((0,), (0,)), ((), ()))
NT = (((1,), (1,)), ((), ()))


def dot(a, b, dims=(((1,), (0,)), ((), ())), precision=None):
    return lax.dot_general(a, b, dims, precision=precision, preferred_element_type=F32)


def live_mask(valid, rows, width):
    return (lax.broadcasted_iota(jnp.int32, (rows, width), 0) < valid).astype(F32).astype(BF16)


def head_column(cum_t, head):
    lane = lax.broadcasted_iota(jnp.int32, cum_t.shape, 1)
    return jnp.sum(jnp.where(lane == head, cum_t, 0.0), axis=1, keepdims=True)


def scan_kernel(
    n, prompt, chunk, group, valid, rate, flags, q_hbm, k_hbm, v_hbm, g_hbm, dq_hbm, dk_hbm, dv_hbm,
    q, k, v, g, dq, dk, dv, cum, cum_t, decay, mask, load, gload, state_bf, grad_bf,
    r_f, r_e, r_b, r_x, r_y, s_x, in_sem, out_sem, send_sem, recv_sem,
):
    rows = q.shape[0]
    size = load.shape[1]
    span = group * size
    groups = load.shape[0] // group
    near = group // chunk
    fetches = ((q_hbm, q), (k_hbm, k), (v_hbm, v), (g_hbm, g))
    results = ((dq, dq_hbm), (dk, dk_hbm), (dv, dv_hbm))

    def columns(part):
        return pl.ds(pl.multiple_of(part * span, span), span)

    def fetch(which, part):
        src, dst = fetches[which]
        return pltpu.make_async_copy(
            src.at[:, columns(part)], dst.at[:, columns(part)], in_sem.at[which, part]
        )

    def store(which, part):
        src, dst = results[which]
        return pltpu.make_async_copy(
            src.at[:, columns(part)], dst.at[:, columns(part)], out_sem.at[which, part]
        )

    for part in range(groups):
        for which in range(4):
            fetch(which, part).start()

    c = lax.axis_index("seq")
    count = load.shape[0] // chunk
    root = prompt - 1
    branch = c >= prompt
    even = lax.rem(c, 2) == 0
    node = branch & even
    inner = node & (c + 4 < n)
    partners = [
        (c > 0, c - 1),
        (c < n - 1, c + 1),
        (inner, c + 4),
        (node & (c - 4 >= prompt), c - 4),
        (c == prompt + 2, root),
        (c == root, prompt + 2),
    ]
    barrier = pltpu.get_barrier_semaphore()
    total = 0
    for cond, other in partners:
        total = total + cond.astype(jnp.int32)

        @pl.when(cond)
        def _(other=other):
            pl.semaphore_signal(
                barrier, inc=1, device_id={"seq": other}, device_id_type=pl.DeviceIdType.MESH
            )

    pl.semaphore_wait(barrier, total)

    def at(i):
        return pl.ds(i * chunk, chunk)

    def copy(src, dst, si, ri, i, other):
        return pltpu.make_async_remote_copy(
            src_ref=src.at[at(i)],
            dst_ref=dst.at[at(i)],
            send_sem=send_sem.at[si, i],
            recv_sem=recv_sem.at[ri, i],
            device_id={"seq": other},
            device_id_type=pl.DeviceIdType.MESH,
        )

    away = lax.rem(c + 1, n)

    def arrived(ref, ri, i):
        copy(ref, ref, 0, ri, i, away).wait_recv()

    sends = [
        ("e", node, r_e, r_e, 1, 1, c + 1),
        ("e", inner, r_e, r_e, 2, 1, c + 4),
        ("f", (c != root) & (c < n - 1), load, r_f, 0, 0, c + 1),
        ("f", c == root, load, r_e, 1, 1, c + 1),
        ("f", c == root, load, r_e, 2, 1, prompt + 2),
        ("b", (c > 0) & (c != prompt), gload, r_b, 3, 2, c - 1),
        ("x", node & (c - 4 >= prompt), s_x, r_x, 4, 3, c - 4),
        ("x", c == prompt, s_x, r_x, 4, 3, c - 1),
        ("x", c == prompt + 2, s_x, r_y, 4, 4, root),
    ]

    def dispatch(kind, i):
        for name, cond, src, dst, si, ri, other in sends:
            if name == kind:

                @pl.when(cond)
                def _(src=src, dst=dst, si=si, ri=ri, other=other):
                    copy(src, dst, si, ri, i, other).start()


    place = lax.broadcasted_iota(jnp.int32, rate.shape, 1)
    log_decay = jnp.where(place < valid[0], -rate[...], 0.0)
    tri = (
        lax.broadcasted_iota(jnp.int32, (rows, rows), 0)
        >= lax.broadcasted_iota(jnp.int32, (rows, rows), 1)
    ).astype(F32)
    high = lax.Precision.HIGHEST
    cum[...] = dot(log_decay, tri, NT, high)
    cum_t[...] = dot(tri, log_decay, NT, high)
    decay[...] = jnp.broadcast_to(jnp.exp(cum[:, rows - 1 : rows]), decay.shape)
    mask[...] = live_mask(valid[0], rows, size)

    def head_columns(head):
        return pl.ds(pl.multiple_of(head * size, size), size)

    def local_states(i):
        for part in range(chunk):
            head = i * chunk + part
            cols = head_columns(head)
            column = head_column(cum_t[...], head)
            head_w = jnp.exp(column)
            tail_w = jnp.exp(column[rows - 1 :, :] - column)
            live = mask[...]
            qm, km, vm, gm = (ref[:, cols] * live for ref in (q, k, v, g))
            q[:, cols] = qm
            k[:, cols] = km
            v[:, cols] = vm
            g[:, cols] = gm
            load[head] = dot((tail_w * km.astype(F32)).astype(BF16), vm, TN)
            gload[head] = dot((head_w * qm.astype(F32)).astype(BF16), gm, TN)

    def block_grads(i):
        for part in range(chunk):
            head = i * chunk + part
            cols = head_columns(head)
            column = head_column(cum_t[...], head)
            row = cum[pl.ds(head, 1), :]
            head_w = jnp.exp(column)
            tail_w = jnp.exp(column[rows - 1 :, :] - column)
            causal_t = lax.broadcasted_iota(jnp.int32, (rows, rows), 0) <= (
                lax.broadcasted_iota(jnp.int32, (rows, rows), 1)
            )
            qm, km, vm, gm = (ref[:, cols] for ref in (q, k, v, g))
            weight_t = jnp.where(causal_t, jnp.exp(jnp.minimum(row - column, 0.0)), 0.0)
            attn_t = (dot(km, qm, NT) * weight_t).astype(BF16)
            gmix_t = (dot(vm, gm, NT) * weight_t).astype(BF16)
            state = state_bf[head]
            grad = grad_bf[head]
            dq[:, cols] = (dot(gmix_t, km, TN) + head_w * dot(gm, state, NT)).astype(BF16)
            dk[:, cols] = (dot(gmix_t, qm) + tail_w * dot(vm, grad, NT)).astype(BF16)
            dv[:, cols] = (dot(attn_t, gm) + tail_w * dot(km, grad)).astype(BF16)

    own = flags[0:1, :][None] > 0.5
    following = flags[1:2, :][None] > 0.5
    zeros = jnp.zeros((chunk,) + load.shape[1:], F32)
    e_depth = jnp.where(even, prompt + (c - prompt) // 4, prompt + (c - 1 - prompt) // 4 + 1)

    def inside(i):
        return (i >= 0) & (i < count)

    def fade(i):
        return jnp.concatenate(
            [decay[pl.ds(i * chunk + j, 1), :][None] for j in range(chunk)], axis=0
        )

    def step(t, carry):
        ie = t - e_depth

        @pl.when(branch & inside(ie))
        def _():
            arrived(r_e, 1, ie)
            dispatch("e", ie)

        i = t - c

        @pl.when(inside(i))
        def _():
            @pl.when((c > 0) & (c != prompt))
            def _():
                arrived(r_f, 0, i)

            @pl.when((c == 0) | (c == prompt))
            def _():
                r_f[at(i)] = zeros

            @pl.when(c < prompt)
            def _():
                r_e[at(i)] = zeros

            state = jnp.where(own, r_e[at(i)], r_f[at(i)])
            load[at(i)] = fade(i) * state + load[at(i)]
            dispatch("f", i)
            state_bf[at(i)] = state.astype(BF16)

        j = t - (n - 1 - c)

        @pl.when(inside(j))
        def _():
            @pl.when((c < n - 1) & (c != root))
            def _():
                arrived(r_b, 2, j)

            @pl.when(c == n - 1)
            def _():
                r_b[at(j)] = zeros

            @pl.when(c == root)
            def _():
                arrived(r_x, 3, j)
                arrived(r_y, 4, j)
                r_b[at(j)] = r_x[at(j)] + r_y[at(j)]

            back = r_b[at(j)]
            held = jnp.where(following, 0.0, back)
            onward = fade(j) * held + gload[at(j)]
            gload[at(j)] = onward
            dispatch("b", j)

            @pl.when(node)
            def _():
                @pl.when(inner)
                def _():
                    arrived(r_x, 3, j)

                @pl.when(jnp.logical_not(inner))
                def _():
                    r_x[at(j)] = zeros

                s_x[at(j)] = (
                    jnp.where(own, onward, 0.0) + jnp.where(following, back, 0.0) + r_x[at(j)]
                )
                dispatch("x", j)

            grad_bf[at(j)] = held.astype(BF16)

        last = t - jnp.maximum(c, n - 1 - c)

        @pl.when(inside(last))
        def _():
            block_grads(last)

            @pl.when(lax.rem(last, near) == near - 1)
            def _():
                for which in range(3):
                    store(which, last // near).start()

        first = t + 1 - jnp.minimum(c, n - 1 - c)

        @pl.when(inside(first))
        def _():
            @pl.when(lax.rem(first, near) == 0)
            def _():
                for which in range(4):
                    fetch(which, first // near).wait()

            local_states(first)

        return carry

    lax.fori_loop(-1, count + n - 1, step, 0)

    def drain(i, carry):
        for name, cond, src, dst, si, ri, other in sends:

            @pl.when(cond)
            def _(src=src, dst=dst, si=si, ri=ri, other=other):
                copy(src, dst, si, ri, i, other).wait_send()

        return carry

    lax.fori_loop(0, count, drain, 0)

    for part in range(groups):
        for which in range(3):
            store(which, part).wait()


def on_device(queries, keys, values, out_grad, decay_rate, block_parent, block_valid):
    rows, width = queries.shape
    heads = decay_rate.shape[0]
    size = width // heads
    n = lax.axis_size("seq")
    prompt = n // 4
    me = lax.axis_index("seq")
    places = jnp.arange(n)
    starts = (places >= prompt) & (block_parent == prompt - 1)
    following = (places == me + 1) & (me != prompt - 1)
    flags = jnp.stack(
        [jnp.any(starts & (places == me)), jnp.any(starts & following)]
    ).astype(F32)
    flags = jnp.broadcast_to(jnp.concatenate([flags, jnp.zeros((6,), F32)])[:, None], (8, size))
    valid = lax.dynamic_slice_in_dim(block_valid, me, 1)

    chunk = 2
    group = 8
    count = heads // chunk
    vmem = pl.BlockSpec(memory_space=pltpu.VMEM)
    hbm = pl.BlockSpec(memory_space=pl.ANY)
    tall = pltpu.VMEM((rows, width), BF16)
    states = pltpu.VMEM((heads, size, size), F32)
    states_bf = pltpu.VMEM((heads, size, size), BF16)
    return pl.pallas_call(
        functools.partial(scan_kernel, n, prompt, chunk, group),
        in_specs=[pl.BlockSpec(memory_space=pltpu.SMEM), vmem, vmem] + [hbm] * 4,
        out_specs=[hbm] * 3,
        out_shape=[jax.ShapeDtypeStruct((rows, width), BF16)] * 3,
        scratch_shapes=[tall] * 7
        + [
            pltpu.VMEM((heads, rows), F32),
            pltpu.VMEM((rows, heads), F32),
            pltpu.VMEM((heads, size), F32),
            pltpu.VMEM((rows, size), BF16),
        ]
        + [states] * 2
        + [states_bf] * 2
        + [states] * 6
        + [
            pltpu.SemaphoreType.DMA((4, heads // group)),
            pltpu.SemaphoreType.DMA((3, heads // group)),
            pltpu.SemaphoreType.DMA((5, count)),
            pltpu.SemaphoreType.DMA((5, count)),
        ],
        compiler_params=pltpu.CompilerParams(
            collective_id=0, has_side_effects=True, vmem_limit_bytes=56 * 2**20
        ),
        name="tree_scan",
    )(valid, decay_rate, flags, queries, keys, values, out_grad)


def solution(mesh):
    rows = P(("groups", "seq"), None)
    placed = (rows, rows, rows, rows, P(None, ("groups", "seq")), P("groups"), P("groups"))
    return jax.shard_map(
        on_device, mesh=mesh, in_specs=placed, out_specs=(rows, rows, rows), check_vma=False
    )
```

```python
import functools

import jax
import jax.numpy as jnp
from jax import lax
from jax.experimental import pallas as pl
from jax.experimental.pallas import tpu as pltpu
from jax.sharding import PartitionSpec as P

F32 = jnp.float32
BF16 = jnp.bfloat16
TN = (((0,), (0,)), ((), ()))
NT = (((1,), (1,)), ((), ()))


def dot(a, b, dims=(((1,), (0,)), ((), ())), precision=None):
    return lax.dot_general(a, b, dims, precision=precision, preferred_element_type=F32)


def live_mask(valid, rows, width):
    return (lax.broadcasted_iota(jnp.int32, (rows, width), 0) < valid).astype(F32).astype(BF16)


def head_column(cum_t, head):
    lane = lax.broadcasted_iota(jnp.int32, cum_t.shape, 1)
    return jnp.sum(jnp.where(lane == head, cum_t, 0.0), axis=1, keepdims=True)


def scan_kernel(
    n, prompt, chunk, group, lag, cut, parent, valid_rows, rate, q_hbm, k_hbm, v_hbm, g_hbm, dq_hbm, dk_hbm, dv_hbm,
    q, k, v, g, dq, dk, dv, cum, cum_t, decay, mask, load, gload, state_bf, grad_bf,
    r_f, r_e, r_b, r_x, r_y, s_x, in_sem, out_sem, send_sem, recv_sem,
):
    rows = q.shape[0]
    size = load.shape[1]
    span = group * size
    groups = load.shape[0] // group
    near = group // chunk
    fetches = ((q_hbm, q), (k_hbm, k), (v_hbm, v), (g_hbm, g))
    results = ((dq, dq_hbm), (dk, dk_hbm), (dv, dv_hbm))

    def columns(part):
        return pl.ds(pl.multiple_of(part * span, span), span)

    def fetch(which, part):
        src, dst = fetches[which]
        return pltpu.make_async_copy(
            src.at[:, columns(part)], dst.at[:, columns(part)], in_sem.at[which, part]
        )

    def store(which, part):
        src, dst = results[which]
        return pltpu.make_async_copy(
            src.at[:, columns(part)], dst.at[:, columns(part)], out_sem.at[which, part]
        )

    for part in range(groups):
        for which in range(4):
            fetch(which, part).start()

    c = lax.axis_index("seq")
    count = load.shape[0] // chunk
    root = prompt - 1
    branch = c >= prompt
    even = lax.rem(c, 2) == 0
    node = branch & even
    inner = node & (c + 4 < n)
    partners = [
        (c > 0, c - 1),
        (c < n - 1, c + 1),
        (inner, c + 4),
        (node & (c - 4 >= prompt), c - 4),
        (c == prompt + 2, root),
        (c == root, prompt + 2),
    ]
    barrier = pltpu.get_barrier_semaphore()
    total = 0
    for cond, other in partners:
        total = total + cond.astype(jnp.int32)

        @pl.when(cond)
        def _(other=other):
            pl.semaphore_signal(
                barrier, inc=1, device_id={"seq": other}, device_id_type=pl.DeviceIdType.MESH
            )

    pl.semaphore_wait(barrier, total)

    def at(i):
        return pl.ds(i * chunk, chunk)

    def copy(src, dst, si, ri, i, other):
        return pltpu.make_async_remote_copy(
            src_ref=src.at[at(i)],
            dst_ref=dst.at[at(i)],
            send_sem=send_sem.at[si, i],
            recv_sem=recv_sem.at[ri, i],
            device_id={"seq": other},
            device_id_type=pl.DeviceIdType.MESH,
        )

    away = lax.rem(c + 1, n)

    def arrived(ref, ri, i):
        copy(ref, ref, 0, ri, i, away).wait_recv()

    sends = [
        ("e", node, r_e, r_e, 1, 1, c + 1),
        ("e", inner, r_e, r_e, 2, 1, c + 4),
        ("f", (c != root) & (c < n - 1), load, r_f, 0, 0, c + 1),
        ("f", c == root, load, r_e, 1, 1, c + 1),
        ("f", c == root, load, r_e, 2, 1, prompt + 2),
        ("b", (c > 0) & (c != prompt), gload, r_b, 3, 2, c - 1),
        ("x", node & (c - 4 >= prompt), s_x, r_x, 4, 3, c - 4),
        ("x", c == prompt, s_x, r_x, 4, 3, c - 1),
        ("x", c == prompt + 2, s_x, r_y, 4, 4, root),
    ]

    def dispatch(kind, i):
        for name, cond, src, dst, si, ri, other in sends:
            if name == kind:

                @pl.when(cond)
                def _(src=src, dst=dst, si=si, ri=ri, other=other):
                    copy(src, dst, si, ri, i, other).start()


    valid = valid_rows[c]
    place = lax.broadcasted_iota(jnp.int32, rate.shape, 1)
    log_decay = jnp.where(place < valid, -rate[...], 0.0)
    tri = (
        lax.broadcasted_iota(jnp.int32, (rows, rows), 0)
        >= lax.broadcasted_iota(jnp.int32, (rows, rows), 1)
    ).astype(F32)
    high = lax.Precision.HIGHEST
    cum[...] = dot(log_decay, tri, NT, high)
    cum_t[...] = dot(tri, log_decay, NT, high)
    decay[...] = jnp.broadcast_to(jnp.exp(cum[:, rows - 1 : rows]), decay.shape)
    mask[...] = live_mask(valid, rows, size)

    def head_columns(head):
        return pl.ds(pl.multiple_of(head * size, size), size)

    def local_states(i):
        for part in range(chunk):
            head = i * chunk + part
            cols = head_columns(head)
            column = head_column(cum_t[...], head)
            head_w = jnp.exp(column)
            tail_w = jnp.exp(column[rows - 1 :, :] - column)
            live = mask[...]
            qm, km, vm, gm = (ref[:, cols] * live for ref in (q, k, v, g))
            q[:, cols] = qm
            k[:, cols] = km
            v[:, cols] = vm
            g[:, cols] = gm
            load[head] = dot((tail_w * km.astype(F32)).astype(BF16), vm, TN)
            gload[head] = dot((head_w * qm.astype(F32)).astype(BF16), gm, TN)

    def block_grads(i):
        for part in range(chunk):
            head = i * chunk + part
            cols = head_columns(head)
            column = head_column(cum_t[...], head)
            row = cum[pl.ds(head, 1), :]
            head_w = jnp.exp(column)
            tail_w = jnp.exp(column[rows - 1 :, :] - column)
            qm, km, vm, gm = (ref[:, cols] for ref in (q, k, v, g))
            inner_q = [None] * (rows // cut)
            inner_k, inner_v = [], []
            for low in range(0, rows, cut):
                here = slice(low, low + cut)
                weight_t = jnp.exp(jnp.minimum(row[:, low:] - column[here], 0.0))
                causal_t = lax.broadcasted_iota(jnp.int32, weight_t.shape, 0) <= (
                    lax.broadcasted_iota(jnp.int32, weight_t.shape, 1)
                )
                weight_t = jnp.where(causal_t, weight_t, 0.0)
                attn_t = (dot(km[here], qm[low:], NT) * weight_t).astype(BF16)
                gmix_t = (dot(vm[here], gm[low:], NT) * weight_t).astype(BF16)
                query_part = dot(gmix_t, km[here], TN)
                for later in range(low, rows, cut):
                    piece = query_part[later - low : later - low + cut]
                    held = inner_q[later // cut]
                    inner_q[later // cut] = piece if held is None else held + piece
                inner_k.append(dot(gmix_t, qm[low:]))
                inner_v.append(dot(attn_t, gm[low:]))
            query_in, key_in, value_in = (
                jnp.concatenate(parts, axis=0) for parts in (inner_q, inner_k, inner_v)
            )
            state = state_bf[head]
            grad = grad_bf[head]
            dq[:, cols] = (query_in + head_w * dot(gm, state, NT)).astype(BF16)
            dk[:, cols] = (key_in + tail_w * dot(vm, grad, NT)).astype(BF16)
            dv[:, cols] = (value_in + tail_w * dot(km, grad)).astype(BF16)

    def starts(block):
        held = parent[jnp.minimum(block, n - 1)]
        here = jnp.where((block >= prompt) & (block < n) & (c != root), root, -2)
        return jnp.full((1, 1, size), held, jnp.int32) == here

    own = starts(c)
    following = starts(c + 1)
    zeros = jnp.zeros((chunk,) + load.shape[1:], F32)
    e_depth = jnp.where(even, prompt + (c - prompt) // 4, prompt + (c - 1 - prompt) // 4 + 1)

    def inside(i):
        return (i >= 0) & (i < count)

    def fade(i):
        return jnp.concatenate(
            [decay[pl.ds(i * chunk + j, 1), :][None] for j in range(chunk)], axis=0
        )

    def step(t, carry):
        ie = t - lag * e_depth

        @pl.when(branch & inside(ie))
        def _():
            arrived(r_e, 1, ie)
            dispatch("e", ie)

        i = t - lag * c

        @pl.when(inside(i))
        def _():
            @pl.when((c > 0) & (c != prompt))
            def _():
                arrived(r_f, 0, i)

            @pl.when((c == 0) | (c == prompt))
            def _():
                r_f[at(i)] = zeros

            @pl.when(c < prompt)
            def _():
                r_e[at(i)] = zeros

            state = jnp.where(own, r_e[at(i)], r_f[at(i)])
            load[at(i)] = fade(i) * state + load[at(i)]
            dispatch("f", i)
            state_bf[at(i)] = state.astype(BF16)

        j = t - lag * (n - 1 - c)

        @pl.when(inside(j))
        def _():
            @pl.when((c < n - 1) & (c != root))
            def _():
                arrived(r_b, 2, j)

            @pl.when(c == n - 1)
            def _():
                r_b[at(j)] = zeros

            @pl.when(c == root)
            def _():
                arrived(r_x, 3, j)
                arrived(r_y, 4, j)
                r_b[at(j)] = r_x[at(j)] + r_y[at(j)]

            back = r_b[at(j)]
            held = jnp.where(following, 0.0, back)
            onward = fade(j) * held + gload[at(j)]
            gload[at(j)] = onward
            dispatch("b", j)

            @pl.when(node)
            def _():
                @pl.when(inner)
                def _():
                    arrived(r_x, 3, j)

                @pl.when(jnp.logical_not(inner))
                def _():
                    r_x[at(j)] = zeros

                s_x[at(j)] = (
                    jnp.where(own, onward, 0.0) + jnp.where(following, back, 0.0) + r_x[at(j)]
                )
                dispatch("x", j)

            grad_bf[at(j)] = held.astype(BF16)

        last = t - lag * jnp.maximum(c, n - 1 - c)

        @pl.when(inside(last))
        def _():
            block_grads(last)

            @pl.when(lax.rem(last, near) == near - 1)
            def _():
                for which in range(3):
                    store(which, last // near).start()

        first = t + 1

        @pl.when(inside(first))
        def _():
            @pl.when(lax.rem(first, near) == 0)
            def _():
                for which in range(4):
                    fetch(which, first // near).wait()

            local_states(first)

        return carry

    lax.fori_loop(-1, count + lag * (n - 1), step, 0)

    def drain(i, carry):
        for name, cond, src, dst, si, ri, other in sends:

            @pl.when(cond)
            def _(src=src, dst=dst, si=si, ri=ri, other=other):
                copy(src, dst, si, ri, i, other).wait_send()

        return carry

    lax.fori_loop(0, count, drain, 0)

    for part in range(groups):
        for which in range(3):
            store(which, part).wait()


def on_device(queries, keys, values, out_grad, decay_rate, block_parent, block_valid):
    rows, width = queries.shape
    heads = decay_rate.shape[0]
    size = width // heads
    n = lax.axis_size("seq")
    prompt = n // 4
    chunk = 1
    group = 8
    lag = 3
    cut = rows
    count = heads // chunk
    smem = pl.BlockSpec(memory_space=pltpu.SMEM)
    vmem = pl.BlockSpec(memory_space=pltpu.VMEM)
    hbm = pl.BlockSpec(memory_space=pl.ANY)
    tall = pltpu.VMEM((rows, width), BF16)
    states = pltpu.VMEM((heads, size, size), F32)
    states_bf = pltpu.VMEM((heads, size, size), BF16)
    return pl.pallas_call(
        functools.partial(scan_kernel, n, prompt, chunk, group, lag, cut),
        in_specs=[smem, smem, vmem] + [hbm] * 4,
        out_specs=[hbm] * 3,
        out_shape=[jax.ShapeDtypeStruct((rows, width), BF16)] * 3,
        scratch_shapes=[tall] * 7
        + [
            pltpu.VMEM((heads, rows), F32),
            pltpu.VMEM((rows, heads), F32),
            pltpu.VMEM((heads, size), F32),
            pltpu.VMEM((rows, size), BF16),
        ]
        + [states] * 2
        + [states_bf] * 2
        + [states] * 6
        + [
            pltpu.SemaphoreType.DMA((4, heads // group)),
            pltpu.SemaphoreType.DMA((3, heads // group)),
            pltpu.SemaphoreType.DMA((5, count)),
            pltpu.SemaphoreType.DMA((5, count)),
        ],
        compiler_params=pltpu.CompilerParams(
            collective_id=0, has_side_effects=True, vmem_limit_bytes=56 * 2**20
        ),
        name="tree_scan",
    )(block_parent, block_valid, decay_rate, queries, keys, values, out_grad)


def solution(mesh):
    rows = P(("groups", "seq"), None)
    placed = (rows, rows, rows, rows, P(None, ("groups", "seq")), P("groups"), P("groups"))
    return jax.shard_map(
        on_device, mesh=mesh, in_specs=placed, out_specs=(rows, rows, rows), check_vma=False
    )
```

```python
import functools

import jax
import jax.numpy as jnp
from jax import lax
from jax.experimental import pallas as pl
from jax.experimental.pallas import tpu as pltpu
from jax.sharding import PartitionSpec as P

F32 = jnp.float32
BF16 = jnp.bfloat16
TN = (((0,), (0,)), ((), ()))
NT = (((1,), (1,)), ((), ()))


def dot(a, b, dims=(((1,), (0,)), ((), ())), precision=None):
    return lax.dot_general(a, b, dims, precision=precision, preferred_element_type=F32)


def live_mask(valid, rows, width):
    return (lax.broadcasted_iota(jnp.int32, (rows, width), 0) < valid).astype(F32).astype(BF16)


def head_column(cum_t, head):
    lane = lax.broadcasted_iota(jnp.int32, cum_t.shape, 1)
    return jnp.sum(jnp.where(lane == head, cum_t, 0.0), axis=1, keepdims=True)


def scan_kernel(
    n, prompt, chunk, group, lag, cut, parent, valid_rows, rate, q_hbm, k_hbm, v_hbm, g_hbm, dq_hbm, dk_hbm, dv_hbm,
    q, k, v, g, dq, dk, dv, cum, cum_t, decay, mask, load, gload, state_bf, grad_bf,
    r_f, r_e, r_b, r_x, r_y, s_x, in_sem, out_sem, send_sem, recv_sem,
):
    rows = q.shape[0]
    size = load.shape[1]
    span = group * size
    groups = load.shape[0] // group
    near = group // chunk
    fetches = ((q_hbm, q), (k_hbm, k), (v_hbm, v), (g_hbm, g))
    results = ((dq, dq_hbm), (dk, dk_hbm), (dv, dv_hbm))

    def columns(part):
        return pl.ds(pl.multiple_of(part * span, span), span)

    def fetch(which, part):
        src, dst = fetches[which]
        return pltpu.make_async_copy(
            src.at[:, columns(part)], dst.at[:, columns(part)], in_sem.at[which, part]
        )

    def store(which, part):
        src, dst = results[which]
        return pltpu.make_async_copy(
            src.at[:, columns(part)], dst.at[:, columns(part)], out_sem.at[which, part]
        )

    for part in range(groups):
        for which in range(4):
            fetch(which, part).start()

    c = lax.axis_index("seq")
    count = load.shape[0] // chunk
    root = prompt - 1
    branch = c >= prompt
    even = lax.rem(c, 2) == 0
    node = branch & even
    inner = node & (c + 4 < n)
    partners = [
        (c > 0, c - 1),
        (c < n - 1, c + 1),
        (inner, c + 4),
        (node & (c - 4 >= prompt), c - 4),
        (c == prompt + 2, root),
        (c == root, prompt + 2),
    ]
    barrier = pltpu.get_barrier_semaphore()
    total = 0
    for cond, other in partners:
        total = total + cond.astype(jnp.int32)

        @pl.when(cond)
        def _(other=other):
            pl.semaphore_signal(
                barrier, inc=1, device_id={"seq": other}, device_id_type=pl.DeviceIdType.MESH
            )

    pl.semaphore_wait(barrier, total)

    def at(i):
        return pl.ds(i * chunk, chunk)

    def copy(src, dst, si, ri, i, other):
        return pltpu.make_async_remote_copy(
            src_ref=src.at[at(i)],
            dst_ref=dst.at[at(i)],
            send_sem=send_sem.at[si, i],
            recv_sem=recv_sem.at[ri, i],
            device_id={"seq": other},
            device_id_type=pl.DeviceIdType.MESH,
        )

    away = lax.rem(c + 1, n)

    def arrived(ref, ri, i):
        copy(ref, ref, 0, ri, i, away).wait_recv()

    sends = [
        ("e", node, r_e, r_e, 1, 1, c + 1),
        ("e", inner, r_e, r_e, 2, 1, c + 4),
        ("f", (c != root) & (c < n - 1), load, r_f, 0, 0, c + 1),
        ("f", c == root, load, r_e, 1, 1, c + 1),
        ("f", c == root, load, r_e, 2, 1, prompt + 2),
        ("b", (c > 0) & (c != prompt), gload, r_b, 3, 2, c - 1),
        ("x", node & (c - 4 >= prompt), s_x, r_x, 4, 3, c - 4),
        ("x", c == prompt, s_x, r_x, 4, 3, c - 1),
        ("x", c == prompt + 2, s_x, r_y, 4, 4, root),
    ]

    def dispatch(kind, i):
        for name, cond, src, dst, si, ri, other in sends:
            if name == kind:

                @pl.when(cond)
                def _(src=src, dst=dst, si=si, ri=ri, other=other):
                    copy(src, dst, si, ri, i, other).start()


    valid = valid_rows[c]
    place = lax.broadcasted_iota(jnp.int32, rate.shape, 1)
    log_decay = jnp.where(place < valid, -rate[...], 0.0)
    tri = (
        lax.broadcasted_iota(jnp.int32, (rows, rows), 0)
        >= lax.broadcasted_iota(jnp.int32, (rows, rows), 1)
    ).astype(F32)
    high = lax.Precision.HIGHEST
    cum[...] = dot(log_decay, tri, NT, high)
    cum_t[...] = dot(tri, log_decay, NT, high)
    decay[...] = jnp.broadcast_to(jnp.exp(cum[:, rows - 1 : rows]), decay.shape)
    mask[...] = live_mask(valid, rows, size)

    def head_columns(head):
        return pl.ds(pl.multiple_of(head * size, size), size)

    def local_states(i):
        for part in range(chunk):
            head = i * chunk + part
            cols = head_columns(head)
            column = head_column(cum_t[...], head)
            head_w = jnp.exp(column)
            tail_w = jnp.exp(column[rows - 1 :, :] - column)
            live = mask[...]
            qm, km, vm, gm = (ref[:, cols] * live for ref in (q, k, v, g))
            q[:, cols] = qm
            k[:, cols] = km
            v[:, cols] = vm
            g[:, cols] = gm
            load[head] = dot((tail_w * km.astype(F32)).astype(BF16), vm, TN)
            gload[head] = dot((head_w * qm.astype(F32)).astype(BF16), gm, TN)

    def block_grads(i):
        for part in range(chunk):
            head = i * chunk + part
            cols = head_columns(head)
            column = head_column(cum_t[...], head)
            row = cum[pl.ds(head, 1), :]
            head_w = jnp.exp(column)
            tail_w = jnp.exp(column[rows - 1 :, :] - column)
            qm, km, vm, gm = (ref[:, cols] for ref in (q, k, v, g))
            inner_q = [None] * (rows // cut)
            inner_k, inner_v = [], []
            for low in range(0, rows, cut):
                here = slice(low, low + cut)
                weight_t = jnp.exp(jnp.minimum(row[:, low:] - column[here], 0.0))
                causal_t = lax.broadcasted_iota(jnp.int32, weight_t.shape, 0) <= (
                    lax.broadcasted_iota(jnp.int32, weight_t.shape, 1)
                )
                weight_t = jnp.where(causal_t, weight_t, 0.0)
                attn_t = (dot(km[here], qm[low:], NT) * weight_t).astype(BF16)
                gmix_t = (dot(vm[here], gm[low:], NT) * weight_t).astype(BF16)
                query_part = dot(gmix_t, km[here], TN)
                for later in range(low, rows, cut):
                    piece = query_part[later - low : later - low + cut]
                    held = inner_q[later // cut]
                    inner_q[later // cut] = piece if held is None else held + piece
                inner_k.append(dot(gmix_t, qm[low:]))
                inner_v.append(dot(attn_t, gm[low:]))
            query_in, key_in, value_in = (
                jnp.concatenate(parts, axis=0) for parts in (inner_q, inner_k, inner_v)
            )
            state = state_bf[head]
            grad = grad_bf[head]
            dq[:, cols] = (query_in + head_w * dot(gm, state, NT)).astype(BF16)
            dk[:, cols] = (key_in + tail_w * dot(vm, grad, NT)).astype(BF16)
            dv[:, cols] = (value_in + tail_w * dot(km, grad)).astype(BF16)

    def starts(block):
        held = parent[jnp.minimum(block, n - 1)]
        here = jnp.where((block >= prompt) & (block < n) & (c != root), root, -2)
        return jnp.full((1, 1, size), held, jnp.int32) == here

    own = starts(c)
    following = starts(c + 1)
    zeros = jnp.zeros((chunk,) + load.shape[1:], F32)
    e_depth = jnp.where(even, prompt + (c - prompt) // 4, prompt + (c - 1 - prompt) // 4 + 1)

    def inside(i):
        return (i >= 0) & (i < count)

    def fade(i):
        return jnp.concatenate(
            [decay[pl.ds(i * chunk + j, 1), :][None] for j in range(chunk)], axis=0
        )

    def step(t, carry):
        ie = t - lag * e_depth

        @pl.when(branch & inside(ie))
        def _():
            arrived(r_e, 1, ie)
            dispatch("e", ie)

        i = t - lag * c

        @pl.when(inside(i))
        def _():
            @pl.when((c > 0) & (c != prompt))
            def _():
                arrived(r_f, 0, i)

            @pl.when((c == 0) | (c == prompt))
            def _():
                r_f[at(i)] = zeros

            @pl.when(c < prompt)
            def _():
                r_e[at(i)] = zeros

            state = jnp.where(own, r_e[at(i)], r_f[at(i)])
            load[at(i)] = fade(i) * state + load[at(i)]
            dispatch("f", i)
            state_bf[at(i)] = state.astype(BF16)

        j = t - lag * (n - 1 - c)

        @pl.when(inside(j))
        def _():
            @pl.when((c < n - 1) & (c != root))
            def _():
                arrived(r_b, 2, j)

            @pl.when(c == n - 1)
            def _():
                r_b[at(j)] = zeros

            @pl.when(c == root)
            def _():
                arrived(r_x, 3, j)
                arrived(r_y, 4, j)
                r_b[at(j)] = r_x[at(j)] + r_y[at(j)]

            back = r_b[at(j)]
            held = jnp.where(following, 0.0, back)
            onward = fade(j) * held + gload[at(j)]
            gload[at(j)] = onward
            dispatch("b", j)

            @pl.when(node)
            def _():
                @pl.when(inner)
                def _():
                    arrived(r_x, 3, j)

                @pl.when(jnp.logical_not(inner))
                def _():
                    r_x[at(j)] = zeros

                s_x[at(j)] = (
                    jnp.where(own, onward, 0.0) + jnp.where(following, back, 0.0) + r_x[at(j)]
                )
                dispatch("x", j)

            grad_bf[at(j)] = held.astype(BF16)

        last = t - lag * (n - 1)

        @pl.when(inside(last))
        def _():
            block_grads(last)

            @pl.when(lax.rem(last, near) == near - 1)
            def _():
                for which in range(3):
                    store(which, last // near).start()

        first = t + 1

        @pl.when(inside(first))
        def _():
            @pl.when(lax.rem(first, near) == 0)
            def _():
                for which in range(4):
                    fetch(which, first // near).wait()

            local_states(first)

        return carry

    lax.fori_loop(-1, count + lag * (n - 1), step, 0)

    def drain(i, carry):
        for name, cond, src, dst, si, ri, other in sends:

            @pl.when(cond)
            def _(src=src, dst=dst, si=si, ri=ri, other=other):
                copy(src, dst, si, ri, i, other).wait_send()

        return carry

    lax.fori_loop(0, count, drain, 0)

    for part in range(groups):
        for which in range(3):
            store(which, part).wait()


def on_device(queries, keys, values, out_grad, decay_rate, block_parent, block_valid):
    rows, width = queries.shape
    heads = decay_rate.shape[0]
    size = width // heads
    n = lax.axis_size("seq")
    prompt = n // 4
    chunk = 1
    group = 8
    lag = 2
    cut = rows
    count = heads // chunk
    smem = pl.BlockSpec(memory_space=pltpu.SMEM)
    vmem = pl.BlockSpec(memory_space=pltpu.VMEM)
    hbm = pl.BlockSpec(memory_space=pl.ANY)
    tall = pltpu.VMEM((rows, width), BF16)
    states = pltpu.VMEM((heads, size, size), F32)
    states_bf = pltpu.VMEM((heads, size, size), BF16)
    return pl.pallas_call(
        functools.partial(scan_kernel, n, prompt, chunk, group, lag, cut),
        in_specs=[smem, smem, vmem] + [hbm] * 4,
        out_specs=[hbm] * 3,
        out_shape=[jax.ShapeDtypeStruct((rows, width), BF16)] * 3,
        scratch_shapes=[tall] * 7
        + [
            pltpu.VMEM((heads, rows), F32),
            pltpu.VMEM((rows, heads), F32),
            pltpu.VMEM((heads, size), F32),
            pltpu.VMEM((rows, size), BF16),
        ]
        + [states] * 2
        + [states_bf] * 2
        + [states] * 6
        + [
            pltpu.SemaphoreType.DMA((4, heads // group)),
            pltpu.SemaphoreType.DMA((3, heads // group)),
            pltpu.SemaphoreType.DMA((5, count)),
            pltpu.SemaphoreType.DMA((5, count)),
        ],
        compiler_params=pltpu.CompilerParams(
            collective_id=0, has_side_effects=True, vmem_limit_bytes=56 * 2**20
        ),
        name="tree_scan",
    )(block_parent, block_valid, decay_rate, queries, keys, values, out_grad)


def solution(mesh):
    rows = P(("groups", "seq"), None)
    placed = (rows, rows, rows, rows, P(None, ("groups", "seq")), P("groups"), P("groups"))
    return jax.shard_map(
        on_device, mesh=mesh, in_specs=placed, out_specs=(rows, rows, rows), check_vma=False
    )
```
